32 devices in a mesh: ctx: 8 (over y, x, core), ch: 4 (over z).
Axes of the slice: x: 2, y: 2, z: 4, core: 2. Of those that a mesh axis runs over, the one named last changes fastest.
Arguments:
- query_in: bfloat16 [1536, 8192], P('ctx', 'ch'), may hold values from -6 to 6
- key_in: bfloat16 [1536, 8192], P('ctx', 'ch'), may hold values from -6 to 6
- value_in: bfloat16 [1536, 8192], P('ctx', 'ch'), may hold values from -6 to 6
- filters: bfloat16 [512, 1536], P('ch'), may hold values from -0.8 to 0.8
- skip_gain: float32 [8192], P('ch'), may hold values from -3 to 3
- out_weight: bfloat16 [8192, 8192], P(None, 'ch'), may hold values from -0.0625 to 0.0625
Outputs:
- output: bfloat16 [1536, 8192], P('ctx', 'ch')
The draws below stay inside these ranges and needn't reach their ends.
All inputs are finite; a program needn't handle non-finite values.
Results may differ from the reference program's by a relative error of at most 0.0057.
Values may be sent and summed in bfloat16 or wider, within the bound.
A program may use at most 128 MiB of HBM per device.

```python
import jax
import jax.numpy as jnp

D = 8192
CG = 16
SEQ = 1536
G = 512


def draw_filters(key, part):
    first, second = jax.random.split(key, 2)
    lowest = 30.0
    spans = jnp.exp(jax.random.uniform(first, (G, 1), jnp.float32, jnp.log(lowest), jnp.log(3.0 * SEQ)))
    lags = jnp.arange(SEQ).astype(jnp.float32)[None, :]
    envelope = jnp.exp(-lags / spans) * jnp.sqrt(2.0 / jnp.minimum(spans, SEQ * 1.0))
    noise = jnp.clip(jax.random.normal(second, (G, SEQ), jnp.float32), -3.0, 3.0)
    return (envelope * noise).astype(jnp.bfloat16)


def shard_levels(rng, dims, shards, least, largest):
    def one(position, blocks):
        steps = jax.random.uniform(jax.random.fold_in(jax.random.fold_in(rng, 6), position), (blocks,), jnp.float32, least / len(shards), largest / len(shards))
        return jnp.repeat(jnp.exp(steps), dims[position] // blocks).reshape((-1,) + (1,) * (len(dims) - position - 1))

    loudness = one(*shards[0])
    for cut in shards[1:]:
        loudness = loudness * one(*cut)
    return loudness


def gaussian(stream_key, extent, deviation, limit, pieces=(), dtype=jnp.bfloat16):
    result = deviation * jax.random.normal(stream_key, extent, jnp.float32)
    if pieces:
        result = result * shard_levels(stream_key, extent, pieces, -0.22, 0.18)
    return jnp.clip(result, -limit, limit).astype(dtype)


def setup_inputs(seed: int = 0) -> dict:
    key_list = jax.random.split(jax.random.key(seed), 7)
    query_in = gaussian(key_list[0], (SEQ, D), 1.0, 6.0, ((0, 8), (1, 4)))
    key_in = gaussian(key_list[1], (SEQ, D), 1.0, 6.0, ((0, 8), (1, 4)))
    value_in = gaussian(key_list[2], (SEQ, D), 1.0, 6.0, ((0, 8), (1, 4)))
    filters = draw_filters(jax.random.fold_in(key_list[6], 71), 0)
    skip_gain = gaussian(key_list[4], (D,), 0.5, 3.0, ((0, 4),), jnp.float32)
    out_weight = gaussian(key_list[5], (D, D), D ** -0.5, 0.0625, ((1, 4),))
    return dict(query_in=query_in, key_in=key_in, value_in=value_in, filters=filters, skip_gain=skip_gain, out_weight=out_weight)


def reference(query_in, key_in, value_in, filters, skip_gain, out_weight):
    mixed = (key_in.astype(jnp.float32) * value_in.astype(jnp.float32)).astype(jnp.bfloat16)
    signal = mixed.astype(jnp.float32).T.reshape(G, CG, SEQ)
    spectrum = jnp.fft.rfft(signal, n=2 * SEQ, axis=-1)
    response = jnp.fft.rfft(filters.astype(jnp.float32), n=2 * SEQ, axis=-1)[:, None, :]
    conv = jnp.fft.irfft(spectrum * response, n=2 * SEQ, axis=-1)[..., :SEQ]
    conv = conv.reshape(D, SEQ).T.astype(jnp.float32)
    direct = skip_gain.astype(jnp.float32)[None, :] * mixed.astype(jnp.float32)
    gated = (query_in.astype(jnp.float32) * (conv + direct)).astype(jnp.bfloat16)
    return jnp.dot(gated, out_weight, preferred_element_type=jnp.float32).astype(jnp.bfloat16)
```

```python
import functools

import jax
import jax.numpy as jnp
from jax import lax
from jax.experimental import pallas as pl
from jax.experimental.pallas import tpu as pltpu
from jax.sharding import PartitionSpec as P

MESH = pl.DeviceIdType.MESH
F32 = jnp.float32
BF16 = jnp.bfloat16
LANES = 128
BLOCK = 256


def kernel(
    J, C, H, sub, width,
    query_ref, key_ref, value_ref, filt_ref, gain_ref, w_hbm, out_ref,
    mixed, mix_send, mix_recv, conv_send, conv_recv, gath, acc, wv, toep, filt32, xt, yt,
    w_sem, ms_sem, mr_sem, cs_sem, cr_sem, zr_sem, zs_sem, zf_sem,
):
    me = lax.axis_index("ctx")
    ch = lax.axis_index("ch")
    rows = query_ref.shape[0]
    seq = J * rows
    narrow = H * sub
    groups = narrow // width
    per = sub // width
    blocks = seq // BLOCK
    right = jnp.minimum(ch + 1, C - 1)
    left = jnp.maximum(ch - 1, 0)
    has_right = ch < C - 1
    has_left = ch > 0

    barrier = pltpu.get_barrier_semaphore()
    for o in range(1, J):
        pl.semaphore_signal(
            barrier, inc=1, device_id=(lax.rem(me + o, J), ch), device_id_type=MESH
        )

    @pl.when(has_right)
    def _():
        pl.semaphore_signal(barrier, inc=1, device_id=(me, right), device_id_type=MESH)

    @pl.when(has_left)
    def _():
        pl.semaphore_signal(barrier, inc=1, device_id=(me, left), device_id_type=MESH)

    def w_copy(s, h):
        return pltpu.make_async_copy(w_hbm.at[s, :, h], wv.at[s, h], w_sem.at[s, h])

    for h in range(H):
        for j in range(J):
            cols = slice(j * narrow + h * sub, j * narrow + (h + 1) * sub)
            part = (key_ref[:, cols].astype(F32) * value_ref[:, cols].astype(F32)).astype(BF16)
            mixed[:, cols] = part
            mix_send[h, j] = part

    pl.semaphore_wait(barrier, J - 1 + has_right.astype(jnp.int32) + has_left.astype(jnp.int32))

    def mix_copy(h, to, frm):
        return pltpu.make_async_remote_copy(
            src_ref=mix_send.at[h, to], dst_ref=mix_recv.at[h, frm],
            send_sem=ms_sem.at[h, to], recv_sem=mr_sem.at[h, frm],
            device_id=(to, ch), device_id_type=MESH,
        )

    def conv_copy(h, to, frm):
        return pltpu.make_async_remote_copy(
            src_ref=conv_send.at[h, to], dst_ref=conv_recv.at[h, frm],
            send_sem=cs_sem.at[h, to], recv_sem=cr_sem.at[h, frm],
            device_id=(to, ch), device_id_type=MESH,
        )

    for h in range(H):
        for o in range(1, J):
            mix_copy(h, lax.rem(me + o, J), me).start()
        mix_recv[h, pl.ds(me, 1)] = mix_send[h, pl.ds(me, 1)]

    for s in range(C):
        for h in range(H):
            w_copy(s, h).start()

    filt32[...] = filt_ref[me].astype(F32)
    toep[:, :, 0:LANES] = jnp.zeros((groups, LANES, LANES), BF16)

    def build(g, carry):
        row = filt32[pl.ds(g, 1), :]
        padded = jnp.concatenate([jnp.zeros((1, LANES), F32), row], axis=1)
        wide = jnp.broadcast_to(padded, (LANES, seq + LANES))
        rolled = pltpu.roll(wide, 0, 1, stride=1, stride_axis=0)
        toep[g, :, LANES:] = rolled[:, LANES:].astype(BF16)
        return carry

    lax.fori_loop(0, groups, build, 0)

    for h in range(H):
        for o in range(1, J):
            mix_copy(h, me, lax.rem(me + o, J)).wait_recv()
        flat = mix_recv[h].reshape(seq, sub)
        xt[...] = flat.T.reshape(per, width, seq)

        def group(g, carry):
            x = xt[g]
            parts = [x[:, b * BLOCK : (b + 1) * BLOCK] for b in range(blocks)]
            sums = [None] * blocks
            for d in range(blocks):
                lhs = jnp.concatenate(parts[: blocks - d], axis=0)
                at = d * BLOCK
                index = h * per + g
                rhs = jnp.concatenate(
                    [
                        toep[index, :, at + LANES : at + LANES + BLOCK],
                        toep[index, :, at : at + BLOCK],
                    ],
                    axis=0,
                )
                res = jnp.dot(lhs, rhs, preferred_element_type=F32)
                for a in range(d, blocks):
                    piece = res[(a - d) * width : (a - d + 1) * width]
                    sums[a] = piece if d == 0 else sums[a] + piece
            yt[g] = jnp.concatenate(sums, axis=1).astype(BF16)
            return carry

        lax.fori_loop(0, per, group, 0)
        back = yt[...].reshape(sub, seq).T
        conv_send[h] = back.reshape(J, rows, sub)
        for o in range(1, J):
            conv_copy(h, lax.rem(me + o, J), me).start()
        conv_recv[h, pl.ds(me, 1)] = conv_send[h, pl.ds(me, 1)]

    def z_copy(s, h, to, sems, way):
        return pltpu.make_async_remote_copy(
            src_ref=gath.at[s, h], dst_ref=gath.at[s, h],
            send_sem=sems.at[s, h], recv_sem=zr_sem.at[s, h],
            device_id=(me, to), device_id_type=MESH,
        )

    def multiply(s, h, first):
        lhs = gath[s, h]
        depth = J * sub
        cols = out_ref.shape[1]
        tile = min(512, cols)

        for n in range(cols // tile):
            at = n * tile
            rhs = wv[s, h, :, :, at : at + tile].reshape(depth, tile)
            res = jnp.dot(lhs, rhs, preferred_element_type=F32)
            if first:
                acc[:, at : at + tile] = res
            else:
                acc[:, at : at + tile] += res

    for h in range(H):
        for o in range(1, J):
            conv_copy(h, me, lax.rem(me + o, J)).wait_recv()
        pieces = []
        for j in range(J):
            cols = slice(j * narrow + h * sub, j * narrow + (h + 1) * sub)
            total = conv_recv[h, j].astype(F32) + gain_ref[:, cols] * mixed[:, cols].astype(F32)
            pieces.append((query_ref[:, cols].astype(F32) * total).astype(BF16))
        gath[pl.ds(ch, 1), h] = jnp.concatenate(pieces, axis=1)[None]

        @pl.when(has_right)
        def _():
            z_copy(ch, h, right, zs_sem, 0).start()

        @pl.when(has_left)
        def _():
            z_copy(ch, h, left, zf_sem, 1).start()

    for s in range(C):
        for h in range(H):
            w_copy(s, h).wait()
    for h in range(H):
        multiply(ch, h, h == 0)

    for step in range(1, C):
        for h in range(H):
            s_left = jnp.maximum(ch - step, 0)

            @pl.when(ch - step >= 0)
            def _():
                z_copy(s_left, h, left, zs_sem, 0).wait_recv()

                @pl.when(has_right)
                def _():
                    z_copy(s_left, h, right, zs_sem, 0).start()

            s_right = jnp.minimum(ch + step, C - 1)

            @pl.when(ch + step < C)
            def _():
                z_copy(s_right, h, right, zf_sem, 1).wait_recv()

                @pl.when(has_left)
                def _():
                    z_copy(s_right, h, left, zf_sem, 1).start()

            @pl.when(ch - step >= 0)
            def _():
                multiply(s_left, h, False)

            @pl.when(ch + step < C)
            def _():
                multiply(s_right, h, False)

    out_ref[...] = acc[...].astype(BF16)

    for h in range(H):
        for o in range(1, J):
            mix_copy(h, lax.rem(me + o, J), me).wait_send()
            conv_copy(h, lax.rem(me + o, J), me).wait_send()
        for s in range(C):

            @pl.when(has_right & (s <= ch))
            def _():
                z_copy(s, h, right, zs_sem, 0).wait_send()

            @pl.when(has_left & (s >= ch))
            def _():
                z_copy(s, h, left, zf_sem, 1).wait_send()


def shards(query_in, key_in, value_in, filters, skip_gain, out_weight):
    J = lax.axis_size("ctx")
    C = lax.axis_size("ch")
    rows, channels = query_in.shape
    seq = J * rows
    width = channels // filters.shape[0]
    narrow = channels // J
    H = 2 if (narrow // width) % 2 == 0 else 1
    sub = narrow // H
    groups = narrow // width
    per = sub // width
    outs = out_weight.shape[1]
    vmem = pl.BlockSpec(memory_space=pltpu.VMEM)
    dma = pltpu.SemaphoreType.DMA
    return pl.pallas_call(
        functools.partial(kernel, J, C, H, sub, width),
        out_shape=jax.ShapeDtypeStruct((rows, outs), BF16),
        in_specs=[vmem] * 5 + [pl.BlockSpec(memory_space=pl.ANY)],
        out_specs=vmem,
        scratch_shapes=[
            pltpu.VMEM((rows, channels), BF16),
            pltpu.VMEM((H, J, rows, sub), BF16),
            pltpu.VMEM((H, J, rows, sub), BF16),
            pltpu.VMEM((H, J, rows, sub), BF16),
            pltpu.VMEM((H, J, rows, sub), BF16),
            pltpu.VMEM((C, H, rows, J * sub), BF16),
            pltpu.VMEM((rows, outs), F32),
            pltpu.VMEM((C, H, J, sub, outs), BF16),
            pltpu.VMEM((groups, LANES, seq + LANES), BF16),
            pltpu.VMEM((groups, seq), F32),
            pltpu.VMEM((per, width, seq), BF16),
            pltpu.VMEM((per, width, seq), BF16),
            dma((C, H)),
            dma((H, J)),
            dma((H, J)),
            dma((H, J)),
            dma((H, J)),
            dma((C, H)),
            dma((C, H)),
            dma((C, H)),
        ],
        compiler_params=pltpu.CompilerParams(
            collective_id=0, has_side_effects=True, vmem_limit_bytes=60 << 20
        ),
        cost_estimate=pl.CostEstimate(
            flops=2 * rows * channels * C * outs,
            bytes_accessed=2 * channels * C * outs,
            transcendentals=0,
        ),
    )(
        query_in, key_in, value_in,
        filters.reshape(J, groups, seq),
        skip_gain.reshape(1, channels),
        out_weight.reshape(C, J, H, sub, outs),
    )


def solution(mesh):
    placed = (P("ctx", "ch"), P("ctx", "ch"), P("ctx", "ch"), P("ch", None), P("ch"), P(None, "ch"))
    return jax.shard_map(
        shards, mesh=mesh, in_specs=placed, out_specs=P("ctx", "ch"), check_vma=False
    )
```

```python
import functools

import jax
import jax.numpy as jnp
from jax import lax
from jax.experimental import pallas as pl
from jax.experimental.pallas import tpu as pltpu
from jax.sharding import PartitionSpec as P

MESH = pl.DeviceIdType.MESH
F32 = jnp.float32
BF16 = jnp.bfloat16
LANES = 128
BLOCK = 256


def kernel(
    J, C, H, sub, width,
    query_ref, key_ref, value_ref, filt_ref, gain_ref, w_hbm, out_ref,
    gcol, mix_send, mix_recv, conv_send, conv_recv, gath, acc, wv, toep, filt32, xt, yt,
    w_sem, ms_sem, mr_sem, cs_sem, cr_sem, zr_sem, zs_sem, zf_sem,
):
    me = lax.axis_index("ctx")
    ch = lax.axis_index("ch")
    rows = query_ref.shape[0]
    seq = J * rows
    narrow = H * sub
    groups = narrow // width
    per = sub // width
    blocks = seq // BLOCK
    right = jnp.minimum(ch + 1, C - 1)
    left = jnp.maximum(ch - 1, 0)
    has_right = ch < C - 1
    has_left = ch > 0

    barrier = pltpu.get_barrier_semaphore()
    for o in range(1, J):
        pl.semaphore_signal(
            barrier, inc=1, device_id=(lax.rem(me + o, J), ch), device_id_type=MESH
        )

    @pl.when(has_right)
    def _():
        pl.semaphore_signal(barrier, inc=1, device_id=(me, right), device_id_type=MESH)

    @pl.when(has_left)
    def _():
        pl.semaphore_signal(barrier, inc=1, device_id=(me, left), device_id_type=MESH)

    def w_copy(s, h):
        return pltpu.make_async_copy(w_hbm.at[s, :, h], wv.at[s, h], w_sem.at[s, h])

    pack = mix_send.shape[3] // sub
    short = rows // pack

    def fold(part):
        cuts = [part[..., i * short : (i + 1) * short, :] for i in range(pack)]
        return jnp.concatenate(cuts, axis=-1) if pack > 1 else part

    def unfold(part):
        cuts = [part[..., i * sub : (i + 1) * sub] for i in range(pack)]
        return jnp.concatenate(cuts, axis=-2) if pack > 1 else part

    def columns(h, j):
        return slice(j * narrow + h * sub, j * narrow + (h + 1) * sub)

    def mix(h):
        for j in range(J):
            cols = columns(h, j)
            part = (key_ref[:, cols].astype(F32) * value_ref[:, cols].astype(F32)).astype(BF16)
            mix_send[h, j] = fold(part)

    def mix_copy(h, to, frm):
        return pltpu.make_async_remote_copy(
            src_ref=mix_send.at[h, to], dst_ref=mix_recv.at[h, frm],
            send_sem=ms_sem.at[h, to], recv_sem=mr_sem.at[h, frm],
            device_id=(to, ch), device_id_type=MESH,
        )

    def conv_copy(h, to, frm):
        return pltpu.make_async_remote_copy(
            src_ref=conv_send.at[h, to], dst_ref=conv_recv.at[h, frm],
            send_sem=cs_sem.at[h, to], recv_sem=cr_sem.at[h, frm],
            device_id=(to, ch), device_id_type=MESH,
        )

    def send_mix(h):
        for o in range(1, J):
            mix_copy(h, lax.rem(me + o, J), me).start()
        mix_recv[h, pl.ds(me, 1)] = mix_send[h, pl.ds(me, 1)]

    mix(0)
    pl.semaphore_wait(barrier, J - 1 + has_right.astype(jnp.int32) + has_left.astype(jnp.int32))

    send_mix(0)
    for h in range(1, H):
        mix(h)
        if h == 1:
            send_mix(1)

    for s in range(C):
        for h in range(H):
            w_copy(s, h).start()

    filt32[...] = filt_ref[me].astype(F32)
    toep[:, :, 0:LANES] = jnp.zeros((groups, LANES, LANES), BF16)
    gain = jnp.broadcast_to(gain_ref[me], (LANES, narrow))
    gcol[...] = gain.T.reshape(groups, width, LANES)

    def build(h):
        for g in range(h * per, (h + 1) * per):
            padded = jnp.concatenate([jnp.zeros((1, LANES), F32), filt32[g : g + 1, :]], axis=1)
            wide = jnp.broadcast_to(padded, (LANES, seq + LANES))
            rolled = pltpu.roll(wide, 0, 1, stride=1, stride_axis=0)
            toep[g, :, LANES:] = rolled[:, LANES:].astype(BF16)

    def convolve(h):
        flat = unfold(mix_recv[h]).reshape(seq, sub)
        xt[...] = flat.T.reshape(per, width, seq)
        for g in range(per):
            index = h * per + g
            x = xt[g]
            parts = [x[:, b * BLOCK : (b + 1) * BLOCK] for b in range(blocks)]
            sums = [None] * blocks
            for d in range(blocks):
                lhs = jnp.concatenate(parts[: blocks - d], axis=0)
                at = d * BLOCK
                rhs = jnp.concatenate(
                    [
                        toep[index, :, at + LANES : at + LANES + BLOCK],
                        toep[index, :, at : at + BLOCK],
                    ],
                    axis=0,
                )
                res = jnp.dot(lhs, rhs, preferred_element_type=F32)
                for a in range(d, blocks):
                    piece = res[(a - d) * width : (a - d + 1) * width]
                    sums[a] = piece if d == 0 else sums[a] + piece
            gain = gcol[index][:, 0:1]
            yt[g] = (jnp.concatenate(sums, axis=1) + gain * x.astype(F32)).astype(BF16)
        back = yt[...].reshape(sub, seq).T
        conv_send[h] = fold(back.reshape(J, rows, sub))
        for o in range(1, J):
            conv_copy(h, lax.rem(me + o, J), me).start()
        conv_recv[h, pl.ds(me, 1)] = conv_send[h, pl.ds(me, 1)]

    def z_copy(s, h, to, sems, way):
        return pltpu.make_async_remote_copy(
            src_ref=gath.at[s, h], dst_ref=gath.at[s, h],
            send_sem=sems.at[s, h], recv_sem=zr_sem.at[s, h],
            device_id=(me, to), device_id_type=MESH,
        )

    def multiply(s, h, first):
        lhs = gath[s, h]
        depth = J * sub
        cols = out_ref.shape[1]
        tile = min(512, cols)

        for n in range(cols // tile):
            at = n * tile
            rhs = wv[s, h, :, :, at : at + tile].reshape(depth, tile)
            res = jnp.dot(lhs, rhs, preferred_element_type=F32)
            if first:
                acc[:, at : at + tile] = res
            else:
                acc[:, at : at + tile] += res

    def gate(h):
        for o in range(1, J):
            conv_copy(h, me, lax.rem(me + o, J)).wait_recv()
        pieces = []
        for j in range(J):
            total = unfold(conv_recv[h, j]).astype(F32)
            pieces.append((query_ref[:, columns(h, j)].astype(F32) * total).astype(BF16))
        gath[pl.ds(ch, 1), h] = jnp.concatenate(pieces, axis=1)[None]

        @pl.when(has_right)
        def _():
            z_copy(ch, h, right, zs_sem, 0).start()

        @pl.when(has_left)
        def _():
            z_copy(ch, h, left, zf_sem, 1).start()

    build(0)
    for h in range(H):
        for o in range(1, J):
            mix_copy(h, me, lax.rem(me + o, J)).wait_recv()
        convolve(h)
        if h + 1 < H:
            if h + 2 < H:
                send_mix(h + 2)
            build(h + 1)
        if h > 0:
            gate(h - 1)
    gate(H - 1)

    for s in range(C):
        for h in range(H):
            w_copy(s, h).wait()
    for h in range(H):
        multiply(ch, h, h == 0)

    for step in range(1, C):
        for h in range(H):
            s_left = jnp.maximum(ch - step, 0)

            @pl.when(ch - step >= 0)
            def _():
                z_copy(s_left, h, left, zs_sem, 0).wait_recv()

                @pl.when(has_right)
                def _():
                    z_copy(s_left, h, right, zs_sem, 0).start()

            s_right = jnp.minimum(ch + step, C - 1)

            @pl.when(ch + step < C)
            def _():
                z_copy(s_right, h, right, zf_sem, 1).wait_recv()

                @pl.when(has_left)
                def _():
                    z_copy(s_right, h, left, zf_sem, 1).start()

            @pl.when(ch - step >= 0)
            def _():
                multiply(s_left, h, False)

            @pl.when(ch + step < C)
            def _():
                multiply(s_right, h, False)

    out_ref[...] = acc[...].astype(BF16)

    for h in range(H):
        for o in range(1, J):
            mix_copy(h, lax.rem(me + o, J), me).wait_send()
            conv_copy(h, lax.rem(me + o, J), me).wait_send()
        for s in range(C):

            @pl.when(has_right & (s <= ch))
            def _():
                z_copy(s, h, right, zs_sem, 0).wait_send()

            @pl.when(has_left & (s >= ch))
            def _():
                z_copy(s, h, left, zf_sem, 1).wait_send()


def shards(query_in, key_in, value_in, filters, skip_gain, out_weight):
    J = lax.axis_size("ctx")
    C = lax.axis_size("ch")
    rows, channels = query_in.shape
    seq = J * rows
    width = channels // filters.shape[0]
    narrow = channels // J
    H = 1
    for cut in (2, 4):
        part = narrow // cut
        fits = LANES % part == 0 and rows % (16 * (LANES // part)) == 0
        if (narrow // width) % cut == 0 and (part % LANES == 0 or fits):
            H = cut
    sub = narrow // H
    pack = max(1, LANES // sub)
    if rows % (16 * pack):
        pack = 1
    groups = narrow // width
    per = sub // width
    outs = out_weight.shape[1]
    vmem = pl.BlockSpec(memory_space=pltpu.VMEM)
    dma = pltpu.SemaphoreType.DMA
    return pl.pallas_call(
        functools.partial(kernel, J, C, H, sub, width),
        out_shape=jax.ShapeDtypeStruct((rows, outs), BF16),
        in_specs=[vmem] * 5 + [pl.BlockSpec(memory_space=pl.ANY)],
        out_specs=vmem,
        scratch_shapes=[
            pltpu.VMEM((groups, width, LANES), F32),
            pltpu.VMEM((H, J, rows // pack, sub * pack), BF16),
            pltpu.VMEM((H, J, rows // pack, sub * pack), BF16),
            pltpu.VMEM((H, J, rows // pack, sub * pack), BF16),
            pltpu.VMEM((H, J, rows // pack, sub * pack), BF16),
            pltpu.VMEM((C, H, rows, J * sub), BF16),
            pltpu.VMEM((rows, outs), F32),
            pltpu.VMEM((C, H, J, sub, outs), BF16),
            pltpu.VMEM((groups, LANES, seq + LANES), BF16),
            pltpu.VMEM((groups, seq), F32),
            pltpu.VMEM((per, width, seq), BF16),
            pltpu.VMEM((per, width, seq), BF16),
            dma((C, H)),
            dma((H, J)),
            dma((H, J)),
            dma((H, J)),
            dma((H, J)),
            dma((C, H)),
            dma((C, H)),
            dma((C, H)),
        ],
        compiler_params=pltpu.CompilerParams(
            collective_id=0, has_side_effects=True, vmem_limit_bytes=60 << 20
        ),
        cost_estimate=pl.CostEstimate(
            flops=2 * rows * channels * C * outs,
            bytes_accessed=2 * channels * C * outs,
            transcendentals=0,
        ),
    )(
        query_in, key_in, value_in,
        filters.reshape(J, groups, seq),
        skip_gain.reshape(J, 1, narrow),
        out_weight.reshape(C, J, H, sub, outs),
    )


def solution(mesh):
    placed = (P("ctx", "ch"), P("ctx", "ch"), P("ctx", "ch"), P("ch", None), P("ch"), P(None, "ch"))
    return jax.shard_map(
        shards, mesh=mesh, in_specs=placed, out_specs=P("ctx", "ch"), check_vma=False
    )
```

```python
import functools

import jax
import jax.numpy as jnp
from jax import lax
from jax.experimental import pallas as pl
from jax.experimental.pallas import tpu as pltpu
from jax.sharding import PartitionSpec as P

MESH = pl.DeviceIdType.MESH
F32 = jnp.float32
BF16 = jnp.bfloat16
LANES = 128
BLOCK = 256


def kernel(
    J, C, H, sub, width,
    query_ref, key_ref, value_ref, filt_ref, gain_ref, w_hbm, out_ref,
    gcol, mix_send, mix_recv, conv_send, conv_recv, gath, acc, wv, toep, filt32, xt, yt,
    w_sem, ms_sem, mr_sem, cs_sem, cr_sem, zr_sem, zs_sem, zf_sem,
):
    me = lax.axis_index("ctx")
    ch = lax.axis_index("ch")
    rows = query_ref.shape[0]
    seq = J * rows
    narrow = H * sub
    groups = narrow // width
    per = sub // width
    blocks = seq // BLOCK
    right = jnp.minimum(ch + 1, C - 1)
    left = jnp.maximum(ch - 1, 0)
    has_right = ch < C - 1
    has_left = ch > 0

    barrier = pltpu.get_barrier_semaphore()
    for o in range(1, J):
        pl.semaphore_signal(
            barrier, inc=1, device_id=(lax.rem(me + o, J), ch), device_id_type=MESH
        )

    @pl.when(has_right)
    def _():
        pl.semaphore_signal(barrier, inc=1, device_id=(me, right), device_id_type=MESH)

    @pl.when(has_left)
    def _():
        pl.semaphore_signal(barrier, inc=1, device_id=(me, left), device_id_type=MESH)

    def w_copy(s, h):
        return pltpu.make_async_copy(w_hbm.at[s, :, h], wv.at[s, h], w_sem.at[s, h])

    pack = mix_send.shape[3] // sub
    short = rows // pack

    def fold(part):
        cuts = [part[..., i * short : (i + 1) * short, :] for i in range(pack)]
        return jnp.concatenate(cuts, axis=-1) if pack > 1 else part

    def unfold(part):
        cuts = [part[..., i * sub : (i + 1) * sub] for i in range(pack)]
        return jnp.concatenate(cuts, axis=-2) if pack > 1 else part

    def columns(h, j):
        return slice(j * narrow + h * sub, j * narrow + (h + 1) * sub)

    def mix(h):
        for j in range(J):
            cols = columns(h, j)
            part = (key_ref[:, cols].astype(F32) * value_ref[:, cols].astype(F32)).astype(BF16)
            mix_send[h, j] = fold(part)

    def mix_copy(h, to, frm):
        return pltpu.make_async_remote_copy(
            src_ref=mix_send.at[h, to], dst_ref=mix_recv.at[h, frm],
            send_sem=ms_sem.at[h, to], recv_sem=mr_sem.at[h, frm],
            device_id=(to, ch), device_id_type=MESH,
        )

    def conv_copy(h, to, frm):
        return pltpu.make_async_remote_copy(
            src_ref=conv_send.at[h, to], dst_ref=conv_recv.at[h, frm],
            send_sem=cs_sem.at[h, to], recv_sem=cr_sem.at[h, frm],
            device_id=(to, ch), device_id_type=MESH,
        )

    def send_mix(h):
        for o in range(1, J):
            mix_copy(h, lax.rem(me + o, J), me).start()
        mix_recv[h, pl.ds(me, 1)] = mix_send[h, pl.ds(me, 1)]

    mix(0)
    pl.semaphore_wait(barrier, J - 1 + has_right.astype(jnp.int32) + has_left.astype(jnp.int32))

    send_mix(0)
    for h in range(1, H):
        mix(h)
        if h == 1:
            send_mix(1)

    for s in range(C):
        for h in range(H):
            w_copy(s, h).start()

    filt32[...] = filt_ref[me].astype(F32)
    toep[:, :, 0:LANES] = jnp.zeros((groups, LANES, LANES), BF16)
    gain = jnp.broadcast_to(gain_ref[me], (LANES, narrow))
    gcol[...] = gain.T.reshape(groups, width, LANES)

    def build(h):
        for g in range(h * per, (h + 1) * per):
            padded = jnp.concatenate([jnp.zeros((1, LANES), F32), filt32[g : g + 1, :]], axis=1)
            wide = jnp.broadcast_to(padded, (LANES, seq + LANES))
            rolled = pltpu.roll(wide, 0, 1, stride=1, stride_axis=0)
            toep[g, :, LANES:] = rolled[:, LANES:].astype(BF16)

    def convolve(h):
        flat = unfold(mix_recv[h]).reshape(seq, sub)
        xt[...] = flat.T.reshape(per, width, seq)
        for g in range(per):
            index = h * per + g
            x = xt[g]
            parts = [x[:, b * BLOCK : (b + 1) * BLOCK] for b in range(blocks)]
            sums = [None] * blocks
            for d in range(blocks):
                lhs = jnp.concatenate(parts[: blocks - d], axis=0)
                at = d * BLOCK
                rhs = jnp.concatenate(
                    [
                        toep[index, :, at + LANES : at + LANES + BLOCK],
                        toep[index, :, at : at + BLOCK],
                    ],
                    axis=0,
                )
                res = jnp.dot(lhs, rhs, preferred_element_type=F32)
                for a in range(d, blocks):
                    piece = res[(a - d) * width : (a - d + 1) * width]
                    sums[a] = piece if d == 0 else sums[a] + piece
            gain = gcol[index][:, 0:1]
            yt[g] = (jnp.concatenate(sums, axis=1) + gain * x.astype(F32)).astype(BF16)
        back = yt[...].reshape(sub, seq).T
        conv_send[h] = fold(back.reshape(J, rows, sub))
        for o in range(1, J):
            conv_copy(h, lax.rem(me + o, J), me).start()
        conv_recv[h, pl.ds(me, 1)] = conv_send[h, pl.ds(me, 1)]

    def z_copy(s, h, to, sems, way):
        return pltpu.make_async_remote_copy(
            src_ref=gath.at[s, h], dst_ref=gath.at[s, h],
            send_sem=sems.at[s, h], recv_sem=zr_sem.at[s, h],
            device_id=(me, to), device_id_type=MESH,
        )

    def multiply(s, h, first):
        lhs = gath[s, h]
        depth = J * sub
        cols = out_ref.shape[1]
        tile = min(512, cols)

        for n in range(cols // tile):
            at = n * tile
            rhs = wv[s, h, :, :, at : at + tile].reshape(depth, tile)
            res = jnp.dot(lhs, rhs, preferred_element_type=F32)
            if first:
                acc[:, at : at + tile] = res
            else:
                acc[:, at : at + tile] += res

    def gate(h):
        for o in range(1, J):
            conv_copy(h, me, lax.rem(me + o, J)).wait_recv()
        pieces = []
        for j in range(J):
            total = unfold(conv_recv[h, j]).astype(F32)
            pieces.append((query_ref[:, columns(h, j)].astype(F32) * total).astype(BF16))
        gath[pl.ds(ch, 1), h] = jnp.concatenate(pieces, axis=1)[None]

        @pl.when(has_right)
        def _():
            z_copy(ch, h, right, zs_sem, 0).start()

        @pl.when(has_left)
        def _():
            z_copy(ch, h, left, zf_sem, 1).start()

    def forward(step, h):
        s_left = jnp.maximum(ch - step, 0)
        s_right = jnp.minimum(ch + step, C - 1)

        @pl.when(ch - step >= 0)
        def _():
            z_copy(s_left, h, left, zs_sem, 0).wait_recv()

            @pl.when(has_right)
            def _():
                z_copy(s_left, h, right, zs_sem, 0).start()

        @pl.when(ch + step < C)
        def _():
            z_copy(s_right, h, right, zf_sem, 1).wait_recv()

            @pl.when(has_left)
            def _():
                z_copy(s_right, h, left, zf_sem, 1).start()

    build(0)
    for h in range(H):
        for o in range(1, J):
            mix_copy(h, me, lax.rem(me + o, J)).wait_recv()
        convolve(h)
        if h + 1 < H:
            if h + 2 < H:
                send_mix(h + 2)
            build(h + 1)
        if h > 0:
            gate(h - 1)
        if h > 2 and C > 1:
            forward(1, h - 3)
    gate(H - 1)

    for s in range(C):
        for h in range(H):
            w_copy(s, h).wait()
    for h in range(H):
        multiply(ch, h, h == 0)

    for step in range(1, C):
        for h in range(H):
            s_left = jnp.maximum(ch - step, 0)
            s_right = jnp.minimum(ch + step, C - 1)
            if step > 1 or h >= max(0, H - 3):
                forward(step, h)

            @pl.when(ch - step >= 0)
            def _():
                multiply(s_left, h, False)

            @pl.when(ch + step < C)
            def _():
                multiply(s_right, h, False)

    out_ref[...] = acc[...].astype(BF16)

    for h in range(H):
        for o in range(1, J):
            mix_copy(h, lax.rem(me + o, J), me).wait_send()
            conv_copy(h, lax.rem(me + o, J), me).wait_send()
        for s in range(C):

            @pl.when(has_right & (s <= ch))
            def _():
                z_copy(s, h, right, zs_sem, 0).wait_send()

            @pl.when(has_left & (s >= ch))
            def _():
                z_copy(s, h, left, zf_sem, 1).wait_send()


def shards(query_in, key_in, value_in, filters, skip_gain, out_weight):
    J = lax.axis_size("ctx")
    C = lax.axis_size("ch")
    rows, channels = query_in.shape
    seq = J * rows
    width = channels // filters.shape[0]
    narrow = channels // J
    H = 1
    for cut in (2, 4, 8):
        part = narrow // cut
        fits = LANES % part == 0 and rows % (16 * (LANES // part)) == 0
        if (narrow // width) % cut == 0 and (part % LANES == 0 or fits):
            H = cut
    sub = narrow // H
    pack = max(1, LANES // sub)
    if rows % (16 * pack):
        pack = 1
    groups = narrow // width
    per = sub // width
    outs = out_weight.shape[1]
    vmem = pl.BlockSpec(memory_space=pltpu.VMEM)
    dma = pltpu.SemaphoreType.DMA
    return pl.pallas_call(
        functools.partial(kernel, J, C, H, sub, width),
        out_shape=jax.ShapeDtypeStruct((rows, outs), BF16),
        in_specs=[vmem] * 5 + [pl.BlockSpec(memory_space=pl.ANY)],
        out_specs=vmem,
        scratch_shapes=[
            pltpu.VMEM((groups, width, LANES), F32),
            pltpu.VMEM((H, J, rows // pack, sub * pack), BF16),
            pltpu.VMEM((H, J, rows // pack, sub * pack), BF16),
            pltpu.VMEM((H, J, rows // pack, sub * pack), BF16),
            pltpu.VMEM((H, J, rows // pack, sub * pack), BF16),
            pltpu.VMEM((C, H, rows, J * sub), BF16),
            pltpu.VMEM((rows, outs), F32),
            pltpu.VMEM((C, H, J, sub, outs), BF16),
            pltpu.VMEM((groups, LANES, seq + LANES), BF16),
            pltpu.VMEM((groups, seq), F32),
            pltpu.VMEM((per, width, seq), BF16),
            pltpu.VMEM((per, width, seq), BF16),
            dma((C, H)),
            dma((H, J)),
            dma((H, J)),
            dma((H, J)),
            dma((H, J)),
            dma((C, H)),
            dma((C, H)),
            dma((C, H)),
        ],
        compiler_params=pltpu.CompilerParams(
            collective_id=0, has_side_effects=True, vmem_limit_bytes=60 << 20
        ),
        cost_estimate=pl.CostEstimate(
            flops=2 * rows * channels * C * outs,
            bytes_accessed=2 * channels * C * outs,
            transcendentals=0,
        ),
    )(
        query_in, key_in, value_in,
        filters.reshape(J, groups, seq),
        skip_gain.reshape(J, 1, narrow),
        out_weight.reshape(C, J, H, sub, outs),
    )


def solution(mesh):
    placed = (P("ctx", "ch"), P("ctx", "ch"), P("ctx", "ch"), P("ch", None), P("ch"), P(None, "ch"))
    return jax.shard_map(
        shards, mesh=mesh, in_specs=placed, out_specs=P("ctx", "ch"), check_vma=False
    )
```
